32 devices in a mesh: leaf: 8 (over z, y), near: 4 (over x, core).
Axes of the slice: x: 2, y: 2, z: 4, core: 2. Of those that a mesh axis runs over, the one named last changes fastest.
Arguments:
- coords: bfloat16 [512, 3, 256], P(('leaf', 'near')), may hold values from 0 to 1
- vectors: float32 [512, 64, 256], P(('leaf', 'near')), may hold values from -6 to 6
- near_list: int32 [512, 16], P(('leaf', 'near')), may hold values from 0 to 511, as said below
- near_count: int32 [512], P(('leaf', 'near')), may hold values from 2 to 16, as said below
- basis_up: float32 [512, 64, 256], P(('leaf', 'near')), may hold values from -0.375 to 0.375
- basis_down: float32 [512, 64, 256], P(('leaf', 'near')), may hold values from -0.75 to 0.75
- up_leaf: float32 [512, 64, 64], P(('leaf', 'near')), may hold values from -0.25 to 0.25
- down_leaf: float32 [512, 64, 64], P(('leaf', 'near')), may hold values from -0.75 to 0.75
- skeleton_box: float32 [64, 3, 64], P(('leaf', 'near')), may hold values from 0 to 1
- far_box: int32 [64, 8], P(('leaf', 'near')), may hold values from 0 to 63, as said below
- up_box: float32 [64, 64, 64], P(('leaf', 'near')), may hold values from -0.5 to 0.5
- down_box: float32 [64, 64, 64], P(('leaf', 'near')), may hold values from -0.75 to 0.75
- skeleton_device: float32 [32, 3, 64], P(('leaf', 'near')), may hold values from 0 to 1
- far_device: int32 [32, 8], P(('leaf', 'near')), may hold values from 0 to 31, as said below
- up_device: float32 [32, 64, 64], P(('leaf', 'near')), may hold values from -0.375 to 0.375
- down_device: float32 [32, 64, 64], P(('leaf', 'near')), may hold values from -0.75 to 0.75
- skeleton_top: float32 [16, 3, 64], replicated, may hold values from 0 to 1
- up_top: float32 [16, 64, 64], replicated, may hold values from -0.5 to 0.5
- down_top: float32 [16, 64, 64], replicated, may hold values from -0.75 to 0.75
Outputs:
- product: float32 [512, 64, 256], P(('leaf', 'near'))
The draws below stay inside these ranges and needn't reach their ends.
Inputs may be any that keep to these rules, and one draw needn't show every extreme that they name: `near_list`: slot 0 of each leaf's list names the leaf itself, and so does every slot at or beyond its count. Every entry names a leaf of a device with the same leaf index (devices are numbered leaf index times 4 plus near index; device d holds leaves 16 d to 16 d + 15). The lists of one device name exactly 4 distinct leaves of each other device with its leaf index. `near_count`: among the devices with one leaf index, some device has all its leaves at 16. `far_box`: each entry names another level-1 box under the same top-tree leaf box (boxes 8 g to 8 g + 7), never the box itself. `far_device`: each entry names a device box other than the box itself.
All inputs are finite; a program needn't handle non-finite values.
Results may differ from the reference program's by a relative error of at most 0.0031.
Values may be sent and summed in bfloat16 or wider, within the bound.
A program may use at most 64 MiB of HBM per device.

```python
import jax
import jax.numpy as jnp
from jax import lax

LEAF = 256
RANK = 64
NRHS = 64
CHILD = 8
BOXES_DEV = 2
NEAR_K = 16
FAR1 = 8
FAR2 = 8
LEAVES_DEV = 16
NEED = 4
NEAR_DEVS = 4
TOP_BOXES = 8
TOP_LEVELS = 3
DEVICE_BOXES = 32
GROUP_BOXES = 8
BOXES = 64
LEAVES = 512
COVER = 1
SPAN_COUNT = 14
HEAP = 16


def near_tables(key):
    device_total = LEAVES // LEAVES_DEV
    request_total = (NEAR_DEVS - 1) * NEED
    pool_size = LEAVES_DEV + request_total

    def pick_leaves(subkey):
        return jax.random.permutation(subkey, LEAVES_DEV)[:NEED].astype(jnp.int32)

    def one_device(device):
        device_key = jax.random.fold_in(jax.random.fold_in(key, 55), device)
        group = device // NEAR_DEVS
        group_key = jax.random.fold_in(jax.random.fold_in(key, 77), group)
        mine = device % NEAR_DEVS
        group_base = group * NEAR_DEVS * LEAVES_DEV
        own_ids = (device * LEAVES_DEV + jnp.arange(LEAVES_DEV, dtype=jnp.int32)).astype(jnp.int32)
        peers = (mine + 1 + jnp.arange(NEAR_DEVS - 1, dtype=jnp.int32)) % NEAR_DEVS
        peer_keys = jax.random.split(jax.random.fold_in(device_key, 1), NEAR_DEVS - 1)
        picked = jax.vmap(pick_leaves)(peer_keys)
        asked_ids = (group_base + peers[:, None] * LEAVES_DEV + picked).reshape(-1).astype(jnp.int32)
        pool_ids = jnp.concatenate([own_ids, asked_ids])
        pool_index = jax.random.randint(jax.random.fold_in(device_key, 2), (LEAVES_DEV, NEAR_K), 0, pool_size)
        random_ids = pool_ids[pool_index]
        slot_index = jnp.arange(NEAR_K, dtype=jnp.int32)[None, :]
        leaf_index = jnp.arange(LEAVES_DEV, dtype=jnp.int32)[:, None]
        cover_index = (slot_index - 1) * LEAVES_DEV + leaf_index
        cover_ids = asked_ids[jnp.clip(cover_index, 0, request_total - 1)]
        use_cover = (slot_index >= 1) & (cover_index < request_total)
        first_factor = jax.random.randint(jax.random.fold_in(device_key, 3), (LEAVES_DEV,), 0, SPAN_COUNT + 1)
        second_factor = jax.random.randint(jax.random.fold_in(device_key, 4), (LEAVES_DEV,), 0, SPAN_COUNT + 1)
        busy_device = jax.random.randint(group_key, (), 0, NEAR_DEVS) == mine
        counts = jnp.where(busy_device, NEAR_K, 1 + COVER + first_factor * second_factor // SPAN_COUNT)
        counts = counts.astype(jnp.int32)
        live_slot = slot_index < counts[:, None]
        entries = jnp.where(use_cover, cover_ids, random_ids)
        entries = jnp.where(live_slot & (slot_index >= 1), entries, own_ids[:, None])
        return (entries.astype(jnp.int32), counts)
    entries, counts = jax.vmap(one_device)(jnp.arange(device_total, dtype=jnp.int32))
    return (entries.reshape(LEAVES, NEAR_K), counts.reshape(LEAVES))


def draw_near_list(key, part):
    return near_tables(key)[0]


def draw_near_count(key, part):
    return near_tables(key)[1]


def draw_far_box(key, part):
    box_total = LEAVES // CHILD
    box_index = jnp.arange(box_total, dtype=jnp.int32)[:, None]
    group = box_index // GROUP_BOXES
    within = box_index % GROUP_BOXES
    shifted = jax.random.randint(key, (box_total, FAR1), 1, GROUP_BOXES)
    return (group * GROUP_BOXES + (within + shifted) % GROUP_BOXES).astype(jnp.int32)


def draw_far_device(key, part):
    device_index = jnp.arange(DEVICE_BOXES, dtype=jnp.int32)[:, None]
    shifted = jax.random.randint(key, (DEVICE_BOXES, FAR2), 1, DEVICE_BOXES)
    return ((device_index + shifted) % DEVICE_BOXES).astype(jnp.int32)


def block_levels(stream_key, dims, cuts, low, high):
    def one(dim, parts):
        heights = jax.random.uniform(jax.random.fold_in(jax.random.fold_in(stream_key, 6), dim), (parts,), jnp.float32, low / len(cuts), high / len(cuts))
        return jnp.repeat(jnp.exp(heights), dims[dim] // parts).reshape((-1,) + (1,) * (len(dims) - dim - 1))

    factor_of = one(*cuts[0])
    for cut in cuts[1:]:
        factor_of = factor_of * one(*cut)
    return factor_of


def centred(own_key, dims, spread, reach, cuts=(), kind=jnp.bfloat16):
    values = jax.random.normal(own_key, dims, jnp.float32) * spread
    if len(cuts) > 0:
        values = block_levels(own_key, dims, cuts, -0.22, 0.18) * values
    return jnp.clip(values, min=-reach, max=reach).astype(kind)


def setup_inputs(seed: int = 0) -> dict:
    splits = jax.random.split(jax.random.key(seed), 20)
    return {
        "coords": jnp.clip(1.0 * jax.random.uniform(splits[0], (LEAVES, 3, LEAF), jnp.float32) ** block_levels(splits[0], (LEAVES, 3, LEAF), ((0, 32),), -0.2, 0.2), 0.0, 1.0).astype(jnp.bfloat16),
        "vectors": centred(splits[1], (LEAVES, NRHS, LEAF), 1.0, 6.0, ((0, 32),), jnp.float32),
        "near_list": draw_near_list(jax.random.fold_in(splits[19], 71), 0),
        "near_count": draw_near_count(jax.random.fold_in(splits[19], 71), 0),
        "basis_up": centred(splits[4], (LEAVES, RANK, LEAF), LEAF ** -0.5, 0.375, ((0, 32),), jnp.float32),
        "basis_down": centred(splits[5], (LEAVES, RANK, LEAF), RANK ** -0.5, 0.75, ((0, 32),), jnp.float32),
        "up_leaf": centred(splits[6], (LEAVES, RANK, RANK), (RANK * CHILD) ** -0.5, 0.25, ((0, 32),), jnp.float32),
        "down_leaf": centred(splits[7], (LEAVES, RANK, RANK), RANK ** -0.5, 0.75, ((0, 32),), jnp.float32),
        "skeleton_box": jnp.clip(1.0 * jax.random.uniform(splits[8], (BOXES, 3, RANK), jnp.float32) ** block_levels(splits[8], (BOXES, 3, RANK), ((0, 32),), -0.2, 0.2), 0.0, 1.0),
        "far_box": draw_far_box(jax.random.fold_in(splits[19], 71), 0),
        "up_box": centred(splits[10], (BOXES, RANK, RANK), (RANK * BOXES_DEV) ** -0.5, 0.5, ((0, 32),), jnp.float32),
        "down_box": centred(splits[11], (BOXES, RANK, RANK), RANK ** -0.5, 0.75, ((0, 32),), jnp.float32),
        "skeleton_device": jnp.clip(1.0 * jax.random.uniform(splits[12], (DEVICE_BOXES, 3, RANK), jnp.float32) ** block_levels(splits[12], (DEVICE_BOXES, 3, RANK), ((0, 32),), -0.2, 0.2), 0.0, 1.0),
        "far_device": draw_far_device(jax.random.fold_in(splits[19], 71), 0),
        "up_device": centred(splits[14], (DEVICE_BOXES, RANK, RANK), (RANK * NEAR_DEVS) ** -0.5, 0.375, ((0, 32),), jnp.float32),
        "down_device": centred(splits[15], (DEVICE_BOXES, RANK, RANK), RANK ** -0.5, 0.75, ((0, 32),), jnp.float32),
        "skeleton_top": jnp.clip(jax.random.uniform(splits[16], (HEAP, 3, RANK), jnp.float32, 0.0, 1.0), 0.0, 1.0),
        "up_top": centred(splits[17], (HEAP, RANK, RANK), (RANK * 2) ** -0.5, 0.5, (), jnp.float32),
        "down_top": centred(splits[18], (HEAP, RANK, RANK), RANK ** -0.5, 0.75, (), jnp.float32),
    }


kernel_scale = 35.0
highest = lax.Precision.HIGHEST


def gaussian(sources, targets):
    summed = None
    for component in range(3):
        offset = sources[..., component, :, None] - targets[..., component, None, :]
        squared = offset * offset
        summed = squared if summed is None else summed + squared
    return jnp.exp(-kernel_scale * summed)


def reference(coords, vectors, near_list, near_count, basis_up, basis_down, up_leaf, down_leaf,
              skeleton_box, far_box, up_box, down_box, skeleton_device, far_device, up_device,
              down_device, skeleton_top, up_top, down_top):
    points = coords.astype(jnp.float32)
    rounded = lax.optimization_barrier(vectors.astype(jnp.bfloat16)).astype(jnp.float32)
    slot_index = jnp.arange(NEAR_K, dtype=jnp.int32)
    live_mask = (slot_index[None, :] < near_count[:, None]).astype(jnp.float32)

    def near_part(pieces):
        targets, source_ids, mask_part = pieces
        kernel = gaussian(points[source_ids], targets[:, None])
        kernel = (kernel * mask_part[:, :, None, None]).astype(jnp.bfloat16)
        kernel = lax.optimization_barrier(kernel).astype(jnp.float32)
        return jnp.einsum('bkns,bkst->bnt', rounded[source_ids], kernel, precision=highest)

    leaf_block = LEAVES_DEV
    near_field = lax.map(near_part, (points.reshape(-1, leaf_block, 3, LEAF),
                                     near_list.reshape(-1, leaf_block, NEAR_K),
                                     live_mask.reshape(-1, leaf_block, NEAR_K)))
    near_field = near_field.reshape(LEAVES, NRHS, LEAF)

    leaf_coeffs = jnp.einsum('lnp,lrp->lnr', vectors, basis_up, precision=highest)
    box_coeffs = jnp.einsum('bcnr,bcrs->bns', leaf_coeffs.reshape(-1, CHILD, NRHS, RANK),
                            up_leaf.reshape(-1, CHILD, RANK, RANK), precision=highest)
    device_coeffs = jnp.einsum('dcnr,dcrs->dns', box_coeffs.reshape(-1, BOXES_DEV, NRHS, RANK),
                               up_box.reshape(-1, BOXES_DEV, RANK, RANK), precision=highest)
    device_terms = jnp.einsum('dnr,drs->dns', device_coeffs, up_device, precision=highest)
    current = jnp.sum(device_terms.reshape(TOP_BOXES, NEAR_DEVS, NRHS, RANK), axis=1)
    couplings = []
    for height in range(TOP_LEVELS):
        box_count = TOP_BOXES >> height
        swapped = current.reshape(box_count // 2, 2, NRHS, RANK)[:, ::-1].reshape(box_count, NRHS, RANK)
        own_skeletons = skeleton_top[box_count:2 * box_count]
        partner_skeletons = own_skeletons.reshape(box_count // 2, 2, 3, RANK)[:, ::-1].reshape(box_count, 3, RANK)
        kernel = gaussian(partner_skeletons, own_skeletons)
        couplings.append(jnp.einsum('bnr,brs->bns', swapped, kernel, precision=highest))
        if height + 1 < TOP_LEVELS:
            product = jnp.einsum('bnr,brs->bns', current, up_top[box_count:2 * box_count], precision=highest)
            product = product.reshape(box_count // 2, 2, NRHS, RANK)
            current = product[:, 0] + product[:, 1]
    top_down = couplings[TOP_LEVELS - 1]
    for height in range(TOP_LEVELS - 2, -1, -1):
        box_count = TOP_BOXES >> height
        parents = jnp.repeat(top_down, 2, axis=0)
        top_down = couplings[height] + jnp.einsum('bnr,brs->bns', parents, down_top[box_count:2 * box_count],
                                                  precision=highest)

    device_kernel = gaussian(skeleton_device[far_device], skeleton_device[:, None])
    device_couple = jnp.einsum('dfnr,dfrs->dns', device_coeffs[far_device], device_kernel, precision=highest)
    box_kernel = gaussian(skeleton_box[far_box], skeleton_box[:, None])
    box_couple = jnp.einsum('bfnr,bfrs->bns', box_coeffs[far_box], box_kernel, precision=highest)
    device_down = device_couple + jnp.einsum('dnr,drs->dns', jnp.repeat(top_down, NEAR_DEVS, axis=0),
                                             down_device, precision=highest)
    box_down = box_couple + jnp.einsum('bnr,brs->bns', jnp.repeat(device_down, BOXES_DEV, axis=0),
                                       down_box, precision=highest)
    leaf_down = jnp.einsum('bnr,brs->bns', jnp.repeat(box_down, CHILD, axis=0), down_leaf, precision=highest)
    far_field = jnp.einsum('lnr,lrp->lnp', leaf_down, basis_down, precision=highest)
    return near_field + far_field
```

```python
import functools
import math

import jax
import jax.numpy as jnp
from jax import lax
from jax.experimental import pallas as pl
from jax.experimental.pallas import tpu as pltpu
from jax.sharding import PartitionSpec as P

kernel_scale = 35.0
exponent_scale = kernel_scale * math.log2(math.e)
f32 = jnp.float32
bf16 = jnp.bfloat16
MESH = pl.DeviceIdType.MESH
NN = (((1,), (0,)), ((), ()))
NT = (((1,), (1,)), ((), ()))


def split(a):
    hi = a.astype(bf16)
    return hi, (a - hi.astype(f32)).astype(bf16)


def dot(a, b, dims=NN):
    return lax.dot_general(a, b, dims, preferred_element_type=f32)


def dot3(a, b, dims=NN):
    (ah, al), (bh, bl) = a, b
    return dot(ah, bh, dims) + (dot(al, bh, dims) + dot(ah, bl, dims))


def kernel(
    G, L, slots, unroll,
    near_ids, box_ids, dev_ids,
    vectors, source, target, basis_up, basis_down, up_leaf, down_leaf,
    up_box, down_box, up_device, down_device, rows, cols, up_top, down_top,
    out,
    table, a_table, box_tab, dev_tab, top_tab,
    tsend, trecv, bsend, brecv, dsend, drecv, fsend, frecv, usend, urecv,
):
    me = lax.axis_index("near")
    ml = lax.axis_index("leaf")
    leaves, columns, size = vectors.shape
    rank = basis_up.shape[1]
    boxes = up_box.shape[0]
    children = leaves // boxes
    levels = L.bit_length() - 1
    partner = me + 1 - 2 * lax.rem(me, 2)
    half = G // 2

    def near_peer(k):
        return lax.rem(me + k, G)

    def leaf_peer(k):
        return lax.rem(ml + k, L)

    def remote(src, dst, send, recv, **where):
        return pltpu.make_async_remote_copy(
            src_ref=src, dst_ref=dst, send_sem=send, recv_sem=recv,
            device_id=where, device_id_type=MESH,
        )

    barrier = pltpu.get_barrier_semaphore()
    for k in range(1, G):
        pl.semaphore_signal(barrier, inc=1, device_id={"near": near_peer(k)}, device_id_type=MESH)
    for k in range(1, L):
        pl.semaphore_signal(barrier, inc=1, device_id={"leaf": leaf_peer(k)}, device_id_type=MESH)

    def stage(l, carry):
        table[me * leaves + l, :columns] = vectors[l].astype(bf16)
        table[me * leaves + l, columns:] = source[l]
        return carry

    lax.fori_loop(0, leaves, stage, 0)
    pl.semaphore_wait(barrier, G - 1 + L - 1)

    def gather(ref, each, send, recv):
        def piece(n):
            return ref.at[pl.ds(n * each, each)]

        mine = piece(me)
        first = [remote(mine, mine, send.at[0], recv.at[0], near=partner)]
        for k in range(1, half):
            first.append(remote(mine, mine, send.at[k], recv.at[k], near=near_peer(2 * k)))
        relay = []
        for k in range(1, half):
            came = piece(lax.rem(me + G - 2 * k, G))
            relay.append(remote(came, came, send.at[half - 1 + k], recv.at[half - 1 + k], near=partner))
        return first, relay

    t_first, t_relay = gather(table, leaves, tsend, trecv)
    for copy in t_first:
        copy.start()

    box_parts = []
    for b in range(boxes):
        total = None
        for c in range(children):
            l = b * children + c
            coeffs = dot3(split(vectors[l]), split(basis_up[l]), NT)
            part = dot3(split(coeffs), split(up_leaf[l]))
            total = part if total is None else total + part
        box_parts.append(split(total))
    device = None
    for b in range(boxes):
        part = dot3(box_parts[b], split(up_box[b]))
        device = part if device is None else device + part
    device = split(device)

    def triple(a):
        hi = a.astype(bf16)
        rest = a - hi.astype(f32)
        mid = rest.astype(bf16)
        return hi, mid, (rest - mid.astype(f32)).astype(bf16)

    triples = triple(rows[:16])
    dev_mine = me * L + ml
    dev_tab[dev_mine, :columns, :rank] = device[0]
    dev_tab[dev_mine, :columns, rank:] = device[1]
    for p in range(3):
        dev_tab[dev_mine, columns + 16 * p:columns + 16 * (p + 1)] = triples[p]
    d_copies = []
    for k in range(1, L):
        spot = dev_tab.at[dev_mine]
        d_copies.append(remote(spot, spot, dsend.at[k - 1], drecv.at[k - 1], leaf=leaf_peer(k)))
        d_copies[-1].start()

    term = split(dot3(device, split(up_device[0])))
    for b in range(boxes):
        box_tab[me, b, :, :rank] = box_parts[b][0]
        box_tab[me, b, :, rank:] = box_parts[b][1]
    box_tab[me, boxes, :, :rank] = term[0]
    box_tab[me, boxes, :, rank:] = term[1]
    for p in range(3):
        box_tab[me, boxes + 1, 16 * p:16 * (p + 1)] = triples[p]
    b_copies = []
    for k in range(1, G):
        spot = box_tab.at[me]
        b_copies.append(remote(spot, spot, bsend.at[k - 1], brecv.at[k - 1], near=near_peer(k)))
        b_copies[-1].start()

    for copy in b_copies:
        copy.wait_recv()
    top = None
    for n in range(G):
        part = box_tab[n, boxes, :, :rank].astype(f32) + box_tab[n, boxes, :, rank:].astype(f32)
        top = part if top is None else top + part
    top = split(top)
    top_tab[ml, :, :rank] = top[0]
    top_tab[ml, :, rank:] = top[1]
    u_copies = []
    for k in range(1, L):
        spot = top_tab.at[ml]
        u_copies.append(remote(spot, spot, usend.at[k - 1], urecv.at[k - 1], leaf=leaf_peer(k)))
        u_copies[-1].start()

    for copy in d_copies:
        copy.wait_recv()
    f_first, f_relay = gather(dev_tab, L, fsend, frecv)
    for copy in f_first:
        copy.start()

    def coupling(row, col):
        summed = None
        for c in range(3):
            offset = col[c] - row[c]
            summed = offset * offset if summed is None else summed + offset * offset
        return split(jnp.exp2(-exponent_scale * summed))

    def own(first):
        return [cols[:, first + c:first + c + 1] for c in range(3)]

    def joined(parts, first):
        whole = (parts[0].astype(f32) + parts[1].astype(f32)) + parts[2].astype(f32)
        return whole[first:first + 3]

    box_down = []
    for b in range(boxes):
        total = None
        for f in range(box_ids.shape[0] // boxes):
            e = box_ids[b * (box_ids.shape[0] // boxes) + f]
            n = lax.shift_right_logical(e, boxes.bit_length() - 1)
            w = jnp.bitwise_and(e, boxes - 1)
            payload = box_tab[n, w]
            skeleton = box_tab[n, boxes + 1]
            whole = joined([skeleton[16 * p:16 * (p + 1)] for p in range(3)], 0)
            whole = jnp.where(w == 0, whole[:, :rank], whole[:, rank:])
            matrix = coupling([whole[c:c + 1] for c in range(3)], own(3 * b))
            part = dot3((payload[:, :rank], payload[:, rank:]), matrix, NT)
            total = part if total is None else total + part
        box_down.append(total)

    for copy in u_copies:
        copy.wait_recv()
    level = [(top_tab[g, :, :rank], top_tab[g, :, rank:]) for g in range(L)]
    couples = []
    for height in range(levels):
        position = jnp.right_shift(ml, height)
        other = jnp.bitwise_xor(position, 1)
        count = L >> height
        chosen = level[0]
        for g in range(1, count):
            chosen = (jnp.where(other == g, level[g][0], chosen[0]),
                      jnp.where(other == g, level[g][1], chosen[1]))
        row = rows[6 + 3 * height:9 + 3 * height, :rank]
        matrix = coupling([row[c:c + 1] for c in range(3)], own(3 * boxes + 3 + 3 * height))
        couples.append(dot3(chosen, matrix, NT))
        if height + 1 < levels:
            moved = [dot3(level[g], split(up_top[count + g])) for g in range(count)]
            level = [split(moved[2 * g] + moved[2 * g + 1]) for g in range(count // 2)]
    top_down = couples[levels - 1]
    for height in range(levels - 2, -1, -1):
        own_id = (L >> height) + jnp.right_shift(ml, height)
        top_down = couples[height] + dot3(split(top_down), split(down_top[own_id]))

    for copy in f_first:
        copy.wait_recv()
    for copy in f_relay:
        copy.start()
    device_down = dot3(split(top_down), split(down_device[0]))
    for copy in f_relay:
        copy.wait_recv()
    for f in range(dev_ids.shape[0]):
        payload = dev_tab[dev_ids[f]]
        whole = joined([payload[columns + 16 * p:columns + 16 * (p + 1)] for p in range(3)], 3)[:, :rank]
        matrix = coupling([whole[c:c + 1] for c in range(3)], own(3 * boxes))
        device_down += dot3((payload[:columns, :rank], payload[:columns, rank:]), matrix, NT)
    device_down = split(device_down)

    for copy in t_first:
        copy.wait_recv()
    for copy in t_relay:
        copy.start()

    for b in range(boxes):
        down = split(box_down[b] + dot3(device_down, split(down_box[b])))
        for c in range(children):
            l = b * children + c
            leaf_down = dot3(down, split(down_leaf[l]))
            out[l] = dot3(split(leaf_down), split(basis_down[l]))

    for copy in t_relay:
        copy.wait_recv()

    def turn(l, carry):
        a_table[l] = table[l, columns:].T
        return carry

    lax.fori_loop(0, G * leaves, turn, 0)
    table[G * leaves] = jnp.zeros(table.shape[1:], bf16)
    a_table[G * leaves] = jnp.zeros(a_table.shape[1:], bf16)

    def one_leaf(l, carry):
        weights = target[l]

        def some_slots(q, total):
            for s in range(unroll):
                e = near_ids[l * slots + q * unroll + s]
                block = jnp.exp2(dot(a_table[e], weights)).astype(bf16)
                total = total + dot(table[e, :columns], block)
            return total

        out[l] = lax.fori_loop(0, slots // unroll, some_slots, out[l])
        return carry

    lax.fori_loop(0, leaves, one_leaf, 0)

    for copy in t_first + t_relay + f_first + f_relay + b_copies + d_copies + u_copies:
        copy.wait_send()


def triple_rows(a):
    hi = lax.reduce_precision(a, 8, 7)
    rest = a - hi
    mid = lax.reduce_precision(rest, 8, 7)
    return [hi, mid, rest - mid]


def on_device(
    coords, vectors, near_list, near_count, basis_up, basis_down, up_leaf, down_leaf,
    skeleton_box, far_box, up_box, down_box, skeleton_device, far_device, up_device,
    down_device, skeleton_top, up_top, down_top,
):
    leaves, _, size = coords.shape
    columns = vectors.shape[1]
    rank = basis_up.shape[1]
    boxes = skeleton_box.shape[0]
    slots = near_list.shape[1]
    G = lax.axis_size("near")
    L = lax.axis_size("leaf")
    levels = L.bit_length() - 1
    ml = lax.axis_index("leaf")

    points = coords.astype(f32)
    norms = -exponent_scale * jnp.sum(points * points, axis=1)
    one = jnp.ones_like(norms)
    none = jnp.zeros_like(norms)
    norm_rows = triple_rows(norms)
    left, right = [], []
    for c in range(3):
        left += [points[:, c]] * 3
        right += triple_rows((2.0 * exponent_scale) * points[:, c])
    left += norm_rows + [one] * 3 + [none]
    right += [one] * 3 + norm_rows + [none]
    source = jnp.stack(left, axis=1).astype(bf16)
    target = jnp.stack(right, axis=1).astype(bf16)

    live = jnp.arange(slots, dtype=jnp.int32)[None] < near_count[:, None]
    near_ids = jnp.where(live, near_list - ml * (G * leaves), G * leaves).reshape(-1)
    box_ids = (far_box - ml * (G * boxes)).reshape(-1)
    dev_ids = ((far_device % G) * L + far_device // G).reshape(-1)

    heights = jnp.arange(levels, dtype=jnp.int32)
    position = jnp.right_shift(ml, heights)
    start = jnp.right_shift(L, heights)
    own_top = skeleton_top[start + position]
    partner_top = skeleton_top[start + jnp.bitwise_xor(position, 1)]
    pad = jnp.zeros((3, 2 * rank - rank), f32)
    box_rows = jnp.concatenate([skeleton_box[b] for b in range(boxes)], axis=1)
    dev_rows = jnp.concatenate([skeleton_device[0], pad], axis=1)
    row_list = [box_rows, dev_rows]
    row_list += [jnp.concatenate([partner_top[h], pad], axis=1) for h in range(levels)]
    all_rows = jnp.concatenate(row_list, axis=0)
    all_rows = jnp.pad(all_rows, ((0, -all_rows.shape[0] % 16), (0, 0)))
    columns_of = jnp.concatenate(
        [skeleton_box.reshape(-1, rank), skeleton_device.reshape(-1, rank), own_top.reshape(-1, rank)], axis=0
    ).T
    columns_of = jnp.pad(columns_of, ((0, 0), (0, 128 - columns_of.shape[1])))

    kinds = [pl.BlockSpec(memory_space=pltpu.SMEM)] * 3 + [pl.BlockSpec(memory_space=pltpu.VMEM)] * 15
    dma = pltpu.SemaphoreType.DMA
    return pl.pallas_call(
        functools.partial(kernel, G, L, slots, 8),
        out_shape=jax.ShapeDtypeStruct(vectors.shape, f32),
        in_specs=kinds,
        out_specs=pl.BlockSpec(memory_space=pltpu.VMEM),
        scratch_shapes=[
            pltpu.VMEM((G * leaves + 1, columns + 16, size), bf16),
            pltpu.VMEM((G * leaves + 1, size, 16), bf16),
            pltpu.VMEM((G, boxes + 2, columns, 2 * rank), bf16),
            pltpu.VMEM((G * L, columns + 48, 2 * rank), bf16),
            pltpu.VMEM((L, columns, 2 * rank), bf16),
            dma((G,)), dma((G,)), dma((G,)), dma((G,)), dma((L,)), dma((L,)),
            dma((G,)), dma((G,)), dma((L,)), dma((L,)),
        ],
        compiler_params=pltpu.CompilerParams(
            collective_id=0, has_side_effects=True, vmem_limit_bytes=56 * 1024 * 1024
        ),
    )(
        near_ids, box_ids, dev_ids, vectors, source, target, basis_up, basis_down, up_leaf, down_leaf,
        up_box, down_box, up_device, down_device, all_rows, columns_of, up_top, down_top,
    )


def solution(mesh):
    split_spec = P(("leaf", "near"))
    return jax.shard_map(
        on_device,
        mesh=mesh,
        in_specs=(split_spec,) * 16 + (P(),) * 3,
        out_specs=split_spec,
        check_vma=False,
    )
```

```python
import functools
import math

import jax
import jax.numpy as jnp
from jax import lax
from jax.experimental import pallas as pl
from jax.experimental.pallas import tpu as pltpu
from jax.sharding import PartitionSpec as P

kernel_scale = 35.0
exponent_scale = kernel_scale * math.log2(math.e)
f32 = jnp.float32
bf16 = jnp.bfloat16
MESH = pl.DeviceIdType.MESH
NN = (((1,), (0,)), ((), ()))
NT = (((1,), (1,)), ((), ()))


def split(a):
    hi = a.astype(bf16)
    return hi, (a - hi.astype(f32)).astype(bf16)


def dot(a, b, dims=NN):
    return lax.dot_general(a, b, dims, preferred_element_type=f32)


def dot3(a, b, dims=NN):
    (ah, al), (bh, bl) = a, b
    return dot(ah, bh, dims) + (dot(al, bh, dims) + dot(ah, bl, dims))


def triple(a):
    hi = a.astype(bf16)
    rest = a - hi.astype(f32)
    mid = rest.astype(bf16)
    return hi, mid, (rest - mid.astype(f32)).astype(bf16)


def kernel(
    G, L, slots, unroll,
    near_list, near_count, far_box, far_device,
    vectors, coords, basis_up, basis_down, up_leaf, down_leaf,
    up_box, down_box, up_device, down_device,
    skeleton_box, skeleton_device, skeleton_top, up_top, down_top,
    out,
    rows, owned, target, table, box_tab, dev_tab, top_tab,
    tsend, trecv, bsend, brecv, dsend, drecv, fsend, frecv, usend, urecv,
):
    me = lax.axis_index("near")
    ml = lax.axis_index("leaf")
    leaves, columns, size = vectors.shape
    rank = basis_up.shape[1]
    boxes = up_box.shape[0]
    children = leaves // boxes
    levels = L.bit_length() - 1
    partner = me + 1 - 2 * lax.rem(me, 2)
    half = G // 2

    def near_peer(k):
        return lax.rem(me + k, G)

    def leaf_peer(k):
        return lax.rem(ml + k, L)

    def remote(src, dst, send, recv, **where):
        return pltpu.make_async_remote_copy(
            src_ref=src, dst_ref=dst, send_sem=send, recv_sem=recv,
            device_id=where, device_id_type=MESH,
        )

    barrier = pltpu.get_barrier_semaphore()
    for k in range(1, G):
        pl.semaphore_signal(barrier, inc=1, device_id={"near": near_peer(k)}, device_id_type=MESH)
    for k in range(1, L):
        pl.semaphore_signal(barrier, inc=1, device_id={"leaf": leaf_peer(k)}, device_id_type=MESH)

    one = jnp.ones((3, size), f32)
    none = jnp.zeros((1, size), f32)

    def stage(l, carry):
        points = coords[l].astype(f32)
        norms = triple(-exponent_scale * jnp.sum(points * points, axis=0, keepdims=True))
        scaled = triple((2.0 * exponent_scale) * points)
        norms = [part.astype(f32) for part in norms]
        scaled = [part.astype(f32) for part in scaled]
        left = jnp.concatenate([points] * 3 + norms + [one, none], axis=0)
        right = jnp.concatenate(scaled + [one] + norms + [none], axis=0)
        table[me * leaves + l, :columns] = vectors[l].astype(bf16)
        table[me * leaves + l, columns:] = left.astype(bf16)
        target[l] = right.astype(bf16)
        return carry

    lax.fori_loop(0, leaves, stage, 0, unroll=4)
    pl.semaphore_wait(barrier, G - 1 + L - 1)

    def gather(ref, each, send, recv):
        def piece(n):
            return ref.at[pl.ds(n * each, each)]

        mine = piece(me)
        first = [remote(mine, mine, send.at[0], recv.at[0], near=partner)]
        for k in range(1, half):
            first.append(remote(mine, mine, send.at[k], recv.at[k], near=near_peer(2 * k)))
        relay = []
        for k in range(1, half):
            came = piece(lax.rem(me + G - 2 * k, G))
            relay.append(remote(came, came, send.at[half - 1 + k], recv.at[half - 1 + k], near=partner))
        return first, relay

    t_first, t_relay = gather(table, leaves, tsend, trecv)
    for copy in t_first:
        copy.start()

    box_parts = []
    for b in range(boxes):
        total = None
        for c in range(children):
            l = b * children + c
            coeffs = dot3(split(vectors[l]), split(basis_up[l]), NT)
            part = dot3(split(coeffs), split(up_leaf[l]))
            total = part if total is None else total + part
        box_parts.append(split(total))
    device = None
    for b in range(boxes):
        part = dot3(box_parts[b], split(up_box[b]))
        device = part if device is None else device + part
    device = split(device)

    rows[...] = jnp.zeros(rows.shape, f32)
    owned[...] = jnp.zeros(owned.shape, f32)
    for b in range(boxes):
        rows[:3, b * rank:(b + 1) * rank] = skeleton_box[b]
        owned[3 * b:3 * b + 3, :rank] = skeleton_box[b]
    rows[3:6, :rank] = skeleton_device[0]
    owned[3 * boxes:3 * boxes + 3, :rank] = skeleton_device[0]
    for height in range(levels):
        first = 3 * boxes + 3 + 3 * height
        owned[first:first + 3, :rank] = skeleton_top[(L >> height) + jnp.right_shift(ml, height)]
    cols = owned[...].T[:rank]
    triples = triple(rows[...])
    dev_mine = me * L + ml
    dev_tab[dev_mine, :columns, :rank] = device[0]
    dev_tab[dev_mine, :columns, rank:] = device[1]
    for p in range(3):
        dev_tab[dev_mine, columns + 16 * p:columns + 16 * (p + 1)] = triples[p]
    d_copies = []
    for k in range(1, L):
        spot = dev_tab.at[dev_mine]
        d_copies.append(remote(spot, spot, dsend.at[k - 1], drecv.at[k - 1], leaf=leaf_peer(k)))
        d_copies[-1].start()

    term = split(dot3(device, split(up_device[0])))
    for b in range(boxes):
        box_tab[me, b, :, :rank] = box_parts[b][0]
        box_tab[me, b, :, rank:] = box_parts[b][1]
    box_tab[me, boxes, :, :rank] = term[0]
    box_tab[me, boxes, :, rank:] = term[1]
    for p in range(3):
        box_tab[me, boxes + 1, 16 * p:16 * (p + 1)] = triples[p]
    b_copies = []
    for k in range(1, G):
        spot = box_tab.at[me]
        b_copies.append(remote(spot, spot, bsend.at[k - 1], brecv.at[k - 1], near=near_peer(k)))
        b_copies[-1].start()

    for copy in b_copies:
        copy.wait_recv()
    top = None
    for n in range(G):
        part = box_tab[n, boxes, :, :rank].astype(f32) + box_tab[n, boxes, :, rank:].astype(f32)
        top = part if top is None else top + part
    top = split(top)
    top_tab[ml, :, :rank] = top[0]
    top_tab[ml, :, rank:] = top[1]
    u_copies = []
    for k in range(1, L):
        spot = top_tab.at[ml]
        u_copies.append(remote(spot, spot, usend.at[k - 1], urecv.at[k - 1], leaf=leaf_peer(k)))
        u_copies[-1].start()

    for copy in d_copies:
        copy.wait_recv()
    f_first, f_relay = gather(dev_tab, L, fsend, frecv)
    for copy in f_first:
        copy.start()

    def coupling(row, col):
        summed = None
        for c in range(3):
            offset = col[c] - row[c]
            summed = offset * offset if summed is None else summed + offset * offset
        return split(jnp.exp2(-exponent_scale * summed))

    def own(first):
        return [cols[:, first + c:first + c + 1] for c in range(3)]

    def joined(parts, first):
        whole = (parts[0].astype(f32) + parts[1].astype(f32)) + parts[2].astype(f32)
        return whole[first:first + 3]

    box_down = []
    for b in range(boxes):
        total = None
        for f in range(far_box.shape[1]):
            e = jnp.bitwise_and(far_box[b, f], G * boxes - 1)
            n = lax.shift_right_logical(e, boxes.bit_length() - 1)
            w = jnp.bitwise_and(e, boxes - 1)
            payload = box_tab[n, w]
            skeleton = box_tab[n, boxes + 1]
            whole = joined([skeleton[16 * p:16 * (p + 1)] for p in range(3)], 0)
            whole = jnp.where(w == 0, whole[:, :rank], whole[:, rank:])
            matrix = coupling([whole[c:c + 1] for c in range(3)], own(3 * b))
            part = dot3((payload[:, :rank], payload[:, rank:]), matrix, NT)
            total = part if total is None else total + part
        box_down.append(total)

    for copy in u_copies:
        copy.wait_recv()
    level = [(top_tab[g, :, :rank], top_tab[g, :, rank:]) for g in range(L)]
    couples = []
    for height in range(levels):
        position = jnp.right_shift(ml, height)
        other = jnp.bitwise_xor(position, 1)
        count = L >> height
        chosen = level[0]
        for g in range(1, count):
            chosen = (jnp.where(other == g, level[g][0], chosen[0]),
                      jnp.where(other == g, level[g][1], chosen[1]))
        row = skeleton_top[count + other]
        matrix = coupling([row[c:c + 1] for c in range(3)], own(3 * boxes + 3 + 3 * height))
        couples.append(dot3(chosen, matrix, NT))
        if height + 1 < levels:
            moved = [dot3(level[g], split(up_top[count + g])) for g in range(count)]
            level = [split(moved[2 * g] + moved[2 * g + 1]) for g in range(count // 2)]
    top_down = couples[levels - 1]
    for height in range(levels - 2, -1, -1):
        own_id = (L >> height) + jnp.right_shift(ml, height)
        top_down = couples[height] + dot3(split(top_down), split(down_top[own_id]))

    for copy in f_first:
        copy.wait_recv()
    for copy in f_relay:
        copy.start()
    device_down = dot3(split(top_down), split(down_device[0]))
    for copy in f_relay:
        copy.wait_recv()
    for f in range(far_device.shape[1]):
        e = far_device[0, f]
        n = jnp.bitwise_and(e, G - 1)
        payload = dev_tab[n * L + jnp.bitwise_and(lax.shift_right_logical(e, G.bit_length() - 1), L - 1)]
        whole = joined([payload[columns + 16 * p:columns + 16 * (p + 1)] for p in range(3)], 3)[:, :rank]
        matrix = coupling([whole[c:c + 1] for c in range(3)], own(3 * boxes))
        device_down += dot3((payload[:columns, :rank], payload[:columns, rank:]), matrix, NT)
    device_down = split(device_down)

    for copy in t_first:
        copy.wait_recv()
    for copy in t_relay:
        copy.start()

    for b in range(boxes):
        down = split(box_down[b] + dot3(device_down, split(down_box[b])))
        for c in range(children):
            l = b * children + c
            leaf_down = dot3(down, split(down_leaf[l]))
            out[l] = dot3(split(leaf_down), split(basis_down[l]))

    for copy in t_relay:
        copy.wait_recv()

    table[G * leaves] = jnp.zeros(table.shape[1:], bf16)

    def one_leaf(l, carry):
        weights = target[l]
        count = near_count[l]

        def some_slots(q, total):
            vals, blks = [], []
            for s in range(unroll):
                slot = q * unroll + s
                e = jnp.where(slot < count, jnp.bitwise_and(near_list[l, slot], G * leaves - 1), G * leaves)
                block = jnp.exp2(dot(table[e, columns:], weights, (((0,), (0,)), ((), ())))).astype(bf16)
                vals.append(table[e, :columns]); blks.append(block)
            for s in range(0, unroll, 8):
                total = total + dot(jnp.concatenate(vals[s:s+8], axis=1), jnp.concatenate(blks[s:s+8], axis=0))
            return total

        out[l] = lax.fori_loop(0, slots // unroll, some_slots, out[l])
        return carry

    lax.fori_loop(0, leaves, one_leaf, 0)

    for copy in t_first + t_relay + f_first + f_relay + b_copies + d_copies + u_copies:
        copy.wait_send()


def on_device(
    coords, vectors, near_list, near_count, basis_up, basis_down, up_leaf, down_leaf,
    skeleton_box, far_box, up_box, down_box, skeleton_device, far_device, up_device,
    down_device, skeleton_top, up_top, down_top,
):
    leaves, _, size = coords.shape
    columns = vectors.shape[1]
    rank = basis_up.shape[1]
    boxes = skeleton_box.shape[0]
    slots = near_list.shape[1]
    G = lax.axis_size("near")
    L = lax.axis_size("leaf")

    kinds = [pl.BlockSpec(memory_space=pltpu.SMEM)] * 4 + [pl.BlockSpec(memory_space=pltpu.VMEM)] * 15
    dma = pltpu.SemaphoreType.DMA
    return pl.pallas_call(
        functools.partial(kernel, G, L, slots, slots),
        out_shape=jax.ShapeDtypeStruct(vectors.shape, f32),
        in_specs=kinds,
        out_specs=pl.BlockSpec(memory_space=pltpu.VMEM),
        scratch_shapes=[
            pltpu.VMEM((16, 2 * rank), f32),
            pltpu.VMEM((32, 2 * rank), f32),
            pltpu.VMEM((leaves, 16, size), bf16),
            pltpu.VMEM((G * leaves + 1, columns + 16, size), bf16),
            pltpu.VMEM((G, boxes + 2, columns, 2 * rank), bf16),
            pltpu.VMEM((G * L, columns + 48, 2 * rank), bf16),
            pltpu.VMEM((L, columns, 2 * rank), bf16),
            dma((G,)), dma((G,)), dma((G,)), dma((G,)), dma((L,)), dma((L,)),
            dma((G,)), dma((G,)), dma((L,)), dma((L,)),
        ],
        compiler_params=pltpu.CompilerParams(
            collective_id=0, has_side_effects=True, vmem_limit_bytes=56 * 1024 * 1024
        ),
    )(
        near_list, near_count, far_box, far_device,
        vectors, coords, basis_up, basis_down, up_leaf, down_leaf,
        up_box, down_box, up_device, down_device,
        skeleton_box, skeleton_device, skeleton_top, up_top, down_top,
    )


def solution(mesh):
    split_spec = P(("leaf", "near"))
    return jax.shard_map(
        on_device,
        mesh=mesh,
        in_specs=(split_spec,) * 16 + (P(),) * 3,
        out_specs=split_spec,
        check_vma=False,
    )
```

```python
import functools
import math

import jax
import jax.numpy as jnp
from jax import lax
from jax.experimental import pallas as pl
from jax.experimental.pallas import tpu as pltpu
from jax.sharding import PartitionSpec as P

kernel_scale = 35.0
exponent_scale = kernel_scale * math.log2(math.e)
f32 = jnp.float32
bf16 = jnp.bfloat16
MESH = pl.DeviceIdType.MESH
NN = (((1,), (0,)), ((), ()))
NT = (((1,), (1,)), ((), ()))


def split(a):
    hi = a.astype(bf16)
    return hi, (a - hi.astype(f32)).astype(bf16)


def dot(a, b, dims=NN):
    return lax.dot_general(a, b, dims, preferred_element_type=f32)


def dot3(a, b, dims=NN):
    (ah, al), (bh, bl) = a, b
    return dot(ah, bh, dims) + (dot(al, bh, dims) + dot(ah, bl, dims))


def triple(a):
    hi = a.astype(bf16)
    rest = a - hi.astype(f32)
    mid = rest.astype(bf16)
    return hi, mid, (rest - mid.astype(f32)).astype(bf16)


def kernel(
    G, L, slots, unroll,
    near_list, near_count, far_box, far_device,
    vectors, coords, basis_up, basis_down, up_leaf, down_leaf,
    up_box, down_box, up_device, down_device,
    skeleton_box, skeleton_device, skeleton_top, up_top, down_top,
    out,
    rows, owned, target, table, box_tab, dev_tab, top_tab,
    tsend, trecv, bsend, brecv, dsend, drecv, fsend, frecv, usend, urecv,
):
    me = lax.axis_index("near")
    ml = lax.axis_index("leaf")
    leaves, columns, size = vectors.shape
    rank = basis_up.shape[1]
    boxes = up_box.shape[0]
    children = leaves // boxes
    levels = L.bit_length() - 1
    partner = me + 1 - 2 * lax.rem(me, 2)
    half = G // 2

    def near_peer(k):
        return lax.rem(me + k, G)

    def leaf_peer(k):
        return lax.rem(ml + k, L)

    def remote(src, dst, send, recv, **where):
        return pltpu.make_async_remote_copy(
            src_ref=src, dst_ref=dst, send_sem=send, recv_sem=recv,
            device_id=where, device_id_type=MESH,
        )

    barrier = pltpu.get_barrier_semaphore()
    for k in range(1, G):
        pl.semaphore_signal(barrier, inc=1, device_id={"near": near_peer(k)}, device_id_type=MESH)
    for k in range(1, L):
        pl.semaphore_signal(barrier, inc=1, device_id={"leaf": leaf_peer(k)}, device_id_type=MESH)

    one = jnp.ones((3, size), f32)
    none = jnp.zeros((1, size), f32)

    def stage(l, carry):
        points = coords[l].astype(f32)
        norms = triple(-exponent_scale * jnp.sum(points * points, axis=0, keepdims=True))
        scaled = triple((2.0 * exponent_scale) * points)
        norms = [part.astype(f32) for part in norms]
        scaled = [part.astype(f32) for part in scaled]
        left = jnp.concatenate([points] * 3 + norms + [one, none], axis=0)
        right = jnp.concatenate(scaled + [one] + norms + [none], axis=0)
        table[me * leaves + l, :columns] = vectors[l].astype(bf16)
        table[me * leaves + l, columns:] = left.astype(bf16)
        target[l] = right.astype(bf16)
        return carry

    lax.fori_loop(0, leaves, stage, 0, unroll=4)
    pl.semaphore_wait(barrier, G - 1 + L - 1)

    def gather(ref, each, send, recv):
        def piece(n):
            return ref.at[pl.ds(n * each, each)]

        mine = piece(me)
        first = [remote(mine, mine, send.at[0], recv.at[0], near=partner)]
        for k in range(1, half):
            first.append(remote(mine, mine, send.at[k], recv.at[k], near=near_peer(2 * k)))
        relay = []
        for k in range(1, half):
            came = piece(lax.rem(me + G - 2 * k, G))
            relay.append(remote(came, came, send.at[half - 1 + k], recv.at[half - 1 + k], near=partner))
        return first, relay

    t_first, t_relay = gather(table, leaves, tsend, trecv)
    for copy in t_first:
        copy.start()

    box_parts = []
    for b in range(boxes):
        total = None
        for c in range(children):
            l = b * children + c
            coeffs = dot3(split(vectors[l]), split(basis_up[l]), NT)
            part = dot3(split(coeffs), split(up_leaf[l]))
            total = part if total is None else total + part
        box_parts.append(split(total))
    device = None
    for b in range(boxes):
        part = dot3(box_parts[b], split(up_box[b]))
        device = part if device is None else device + part
    device = split(device)

    rows[...] = jnp.zeros(rows.shape, f32)
    owned[...] = jnp.zeros(owned.shape, f32)
    for b in range(boxes):
        rows[:3, b * rank:(b + 1) * rank] = skeleton_box[b]
        owned[3 * b:3 * b + 3, :rank] = skeleton_box[b]
    rows[3:6, :rank] = skeleton_device[0]
    owned[3 * boxes:3 * boxes + 3, :rank] = skeleton_device[0]
    for height in range(levels):
        first = 3 * boxes + 3 + 3 * height
        owned[first:first + 3, :rank] = skeleton_top[(L >> height) + jnp.right_shift(ml, height)]
    cols = owned[...].T[:rank]
    triples = triple(rows[...])
    dev_mine = me * L + ml
    dev_tab[dev_mine, :columns, :rank] = device[0]
    dev_tab[dev_mine, :columns, rank:] = device[1]
    packed = [part.astype(f32)[3:6] for part in triples] + [jnp.zeros((7, 2 * rank), f32)]
    dev_tab[dev_mine, columns:] = jnp.concatenate(packed, axis=0).astype(bf16)
    d_copies = []
    for k in range(1, L):
        spot = dev_tab.at[dev_mine]
        d_copies.append(remote(spot, spot, dsend.at[k - 1], drecv.at[k - 1], leaf=leaf_peer(k)))
        d_copies[-1].start()

    term = split(dot3(device, split(up_device[0])))
    for b in range(boxes):
        box_tab[me, b, :, :rank] = box_parts[b][0]
        box_tab[me, b, :, rank:] = box_parts[b][1]
    box_tab[me, boxes, :, :rank] = term[0]
    box_tab[me, boxes, :, rank:] = term[1]
    for p in range(3):
        box_tab[me, boxes + 1, 16 * p:16 * (p + 1)] = triples[p]
    b_copies = []
    for k in range(1, G):
        spot = box_tab.at[me]
        b_copies.append(remote(spot, spot, bsend.at[k - 1], brecv.at[k - 1], near=near_peer(k)))
        b_copies[-1].start()

    for copy in b_copies:
        copy.wait_recv()
    top = None
    for n in range(G):
        part = box_tab[n, boxes, :, :rank].astype(f32) + box_tab[n, boxes, :, rank:].astype(f32)
        top = part if top is None else top + part
    top = split(top)
    top_tab[ml, :, :rank] = top[0]
    top_tab[ml, :, rank:] = top[1]
    u_copies = []
    for k in range(1, L):
        spot = top_tab.at[ml]
        u_copies.append(remote(spot, spot, usend.at[k - 1], urecv.at[k - 1], leaf=leaf_peer(k)))
        u_copies[-1].start()

    for copy in d_copies:
        copy.wait_recv()
    f_first, f_relay = gather(dev_tab, L, fsend, frecv)
    for copy in f_first:
        copy.start()

    def coupling(row, col):
        summed = None
        for c in range(3):
            offset = col[c] - row[c]
            summed = offset * offset if summed is None else summed + offset * offset
        return split(jnp.exp2(-exponent_scale * summed))

    def own(first):
        return [cols[:, first + c:first + c + 1] for c in range(3)]

    def joined(parts):
        whole = (parts[0].astype(f32) + parts[1].astype(f32)) + parts[2].astype(f32)
        return whole[:3]

    box_down = []
    for b in range(boxes):
        total = None
        for f in range(far_box.shape[1]):
            e = jnp.bitwise_and(far_box[b, f], G * boxes - 1)
            n = lax.shift_right_logical(e, boxes.bit_length() - 1)
            w = jnp.bitwise_and(e, boxes - 1)
            payload = box_tab[n, w]
            skeleton = box_tab[n, boxes + 1]
            whole = joined([skeleton[16 * p:16 * (p + 1)] for p in range(3)])
            whole = jnp.where(w == 0, whole[:, :rank], whole[:, rank:])
            matrix = coupling([whole[c:c + 1] for c in range(3)], own(3 * b))
            part = dot3((payload[:, :rank], payload[:, rank:]), matrix, NT)
            total = part if total is None else total + part
        box_down.append(total)

    for copy in u_copies:
        copy.wait_recv()
    level = [(top_tab[g, :, :rank], top_tab[g, :, rank:]) for g in range(L)]
    couples = []
    for height in range(levels):
        position = jnp.right_shift(ml, height)
        other = jnp.bitwise_xor(position, 1)
        count = L >> height
        chosen = level[0]
        for g in range(1, count):
            chosen = (jnp.where(other == g, level[g][0], chosen[0]),
                      jnp.where(other == g, level[g][1], chosen[1]))
        row = skeleton_top[count + other]
        matrix = coupling([row[c:c + 1] for c in range(3)], own(3 * boxes + 3 + 3 * height))
        couples.append(dot3(chosen, matrix, NT))
        if height + 1 < levels:
            moved = [dot3(level[g], split(up_top[count + g])) for g in range(count)]
            level = [split(moved[2 * g] + moved[2 * g + 1]) for g in range(count // 2)]
    top_down = couples[levels - 1]
    for height in range(levels - 2, -1, -1):
        own_id = (L >> height) + jnp.right_shift(ml, height)
        top_down = couples[height] + dot3(split(top_down), split(down_top[own_id]))

    for copy in f_first:
        copy.wait_recv()
    for copy in f_relay:
        copy.start()
    device_down = dot3(split(top_down), split(down_device[0]))
    for copy in f_relay:
        copy.wait_recv()
    for f in range(far_device.shape[1]):
        e = far_device[0, f]
        n = jnp.bitwise_and(e, G - 1)
        payload = dev_tab[n * L + jnp.bitwise_and(lax.shift_right_logical(e, G.bit_length() - 1), L - 1)]
        whole = payload[columns:].astype(f32)[:, :rank]
        whole = (whole[:3] + whole[3:6]) + whole[6:9]
        matrix = coupling([whole[c:c + 1] for c in range(3)], own(3 * boxes))
        device_down += dot3((payload[:columns, :rank], payload[:columns, rank:]), matrix, NT)
    device_down = split(device_down)

    for copy in t_first:
        copy.wait_recv()
    for copy in t_relay:
        copy.start()

    for b in range(boxes):
        down = split(box_down[b] + dot3(device_down, split(down_box[b])))
        for c in range(children):
            l = b * children + c
            leaf_down = dot3(down, split(down_leaf[l]))
            out[l] = dot3(split(leaf_down), split(basis_down[l]))

    for copy in t_relay:
        copy.wait_recv()

    table[G * leaves] = jnp.zeros(table.shape[1:], bf16)

    def one_leaf(l, carry):
        weights = target[l]
        count = near_count[l]

        def some_slots(q, total):
            vals, blks = [], []
            for s in range(unroll):
                slot = q * unroll + s
                e = jnp.where(slot < count, jnp.bitwise_and(near_list[l, slot], G * leaves - 1), G * leaves)
                block = jnp.exp2(dot(table[e, columns:], weights, (((0,), (0,)), ((), ())))).astype(bf16)
                vals.append(table[e, :columns]); blks.append(block)
            for s in range(0, unroll, 8):
                total = total + dot(jnp.concatenate(vals[s:s+8], axis=1), jnp.concatenate(blks[s:s+8], axis=0))
            return total

        out[l] = lax.fori_loop(0, slots // unroll, some_slots, out[l])
        return carry

    lax.fori_loop(0, leaves, one_leaf, 0)

    for copy in t_first + t_relay + f_first + f_relay + b_copies + d_copies + u_copies:
        copy.wait_send()


def on_device(
    coords, vectors, near_list, near_count, basis_up, basis_down, up_leaf, down_leaf,
    skeleton_box, far_box, up_box, down_box, skeleton_device, far_device, up_device,
    down_device, skeleton_top, up_top, down_top,
):
    leaves, _, size = coords.shape
    columns = vectors.shape[1]
    rank = basis_up.shape[1]
    boxes = skeleton_box.shape[0]
    slots = near_list.shape[1]
    G = lax.axis_size("near")
    L = lax.axis_size("leaf")

    kinds = [pl.BlockSpec(memory_space=pltpu.SMEM)] * 4 + [pl.BlockSpec(memory_space=pltpu.VMEM)] * 15
    dma = pltpu.SemaphoreType.DMA
    return pl.pallas_call(
        functools.partial(kernel, G, L, slots, slots),
        out_shape=jax.ShapeDtypeStruct(vectors.shape, f32),
        in_specs=kinds,
        out_specs=pl.BlockSpec(memory_space=pltpu.VMEM),
        scratch_shapes=[
            pltpu.VMEM((16, 2 * rank), f32),
            pltpu.VMEM((32, 2 * rank), f32),
            pltpu.VMEM((leaves, 16, size), bf16),
            pltpu.VMEM((G * leaves + 1, columns + 16, size), bf16),
            pltpu.VMEM((G, boxes + 2, columns, 2 * rank), bf16),
            pltpu.VMEM((G * L, columns + 16, 2 * rank), bf16),
            pltpu.VMEM((L, columns, 2 * rank), bf16),
            dma((G,)), dma((G,)), dma((G,)), dma((G,)), dma((L,)), dma((L,)),
            dma((G,)), dma((G,)), dma((L,)), dma((L,)),
        ],
        compiler_params=pltpu.CompilerParams(
            collective_id=0, has_side_effects=True, vmem_limit_bytes=56 * 1024 * 1024
        ),
    )(
        near_list, near_count, far_box, far_device,
        vectors, coords, basis_up, basis_down, up_leaf, down_leaf,
        up_box, down_box, up_device, down_device,
        skeleton_box, skeleton_device, skeleton_top, up_top, down_top,
    )


def solution(mesh):
    split_spec = P(("leaf", "near"))
    return jax.shard_map(
        on_device,
        mesh=mesh,
        in_specs=(split_spec,) * 16 + (P(),) * 3,
        out_specs=split_spec,
        check_vma=False,
    )
```
